128 devices in a mesh: blk: 32 (over x, z_hi, y), frq: 4 (over z_lo, core).
Axes of the slice: x: 4, y: 4, z: 4 (z_hi: 2, z_lo: 2; z = z_hi * 2 + z_lo), core: 2. Of those that a mesh axis runs over, the one named last changes fastest.
Arguments:
- spectra: bfloat16 [2, 4096, 64, 512], P(None, 'blk', None, 'frq'), may hold values from -6 to 6
- live: int32 [4096], P('blk'), may hold values 0 or 1
Outputs:
- xcorr: float32 [3, 4096, 128, 128], P(None, ('blk', 'frq'))
The draws below stay inside these ranges and needn't reach their ends.
All inputs are finite; a program needn't handle non-finite values. No bound on the sum of `live` on one device may be relied on, other than what follows from the above.
Results may differ from the reference program's by a relative error of at most 0.0058.
Values may be sent and summed in bfloat16 or wider, within the bound.
A program may use at most 128 MiB of HBM per device.

```python
import math
import jax
import jax.numpy as jnp
from jax import lax

BLOCK = 128
F = 512
W = 64
LAGS = 128
ROUNDS = 3
NCH = 4096
N_BLK = 32


def with_ends(result, own_key, least, largest):
    shape = result.shape
    spot = [jax.random.randint(jax.random.fold_in(own_key, axis), (), 0, shape[axis]) for axis in range(len(shape))]
    result = result.at[tuple(spot)].set(least)
    longest = shape.index(max(shape))
    spot[longest] = (spot[longest] + 1) % shape[longest]
    return result.at[tuple(spot)].set(largest)


def level_of(own_key, shape, split, least, largest):
    loudness = 1.0
    for axis_at, blocks in split:
        heights = jax.random.uniform(jax.random.fold_in(jax.random.fold_in(own_key, 6), axis_at), (blocks,), jnp.float32, least / len(split), largest / len(split))
        loudness = loudness * jnp.repeat(jnp.exp(heights), shape[axis_at] // blocks).reshape((-1,) + (1,) * (len(shape) - 1 - axis_at))
    return loudness


def scatter_about(rng, shape, deviation, bound, split=(), held_as=jnp.bfloat16):
    drawn = deviation * jax.random.normal(rng, shape, jnp.float32)
    if split:
        drawn = drawn * level_of(rng, shape, split, -0.22, 0.18)
    return jnp.clip(drawn, -bound, bound).astype(held_as)


def setup_inputs(seed: int = 0) -> dict:
    key_list = jax.random.split(jax.random.key(seed), 3)
    return {
        "spectra": scatter_about(key_list[0], (2, NCH, W, F), 1.0, 6.0, ((1, 32), (3, 4))),
        "live": with_ends((jax.random.randint(key_list[1], (NCH,), 0, 8) < 7).astype(jnp.int32), jax.random.fold_in(key_list[1], 1), 0, 1),
    }


EPSILON = 1e-06

def normalize(spectra, live):
    values = spectra.astype(jnp.float32)
    energy = lax.optimization_barrier(jnp.mean(values * values, axis=(0, 2), keepdims=True))
    weight = live.astype(jnp.float32)[None, :, None, None] * lax.rsqrt(energy + EPSILON)
    return (values * weight).astype(jnp.bfloat16)

def lag_table(first_bin, bin_count, length_all, lag_count):
    bins = first_bin + jnp.arange(bin_count, dtype=jnp.int32)
    delays = jnp.arange(lag_count, dtype=jnp.int32) - lag_count // 2
    residue = jnp.mod(bins[:, None] * delays[None, :], 2 * length_all)
    phases = residue.astype(jnp.float32) * (math.pi / length_all)
    factor = 1.0 / math.sqrt(length_all)
    return jnp.stack([jnp.cos(phases) * factor, -jnp.sin(phases) * factor], 0).astype(jnp.bfloat16)

def cross_block(local_block, remote_block):
    local_f = local_block.astype(jnp.float32)
    remote_f = remote_block.astype(jnp.float32)

    def product(left, right):
        return jnp.einsum('cwf,dwf->cdf', left, right)
    factor = 1.0 / math.sqrt(W)
    real_part = (product(local_f[0], remote_f[0]) + product(local_f[1], remote_f[1])) * factor
    imag_part = (product(local_f[1], remote_f[0]) - product(local_f[0], remote_f[1])) * factor
    return jnp.stack([real_part, imag_part], axis=2).astype(jnp.bfloat16)

def reference(spectra, live):
    normed = normalize(spectra, live)
    full_table = lag_table(0, F, F, LAGS).reshape(2 * F, LAGS)
    blocks = normed.reshape(2, N_BLK, BLOCK, W, F).transpose(1, 0, 2, 3, 4)
    results = []
    for offset in range(1, ROUNDS + 1):
        partner = jnp.roll(blocks, -offset, axis=0)

        def one_couple(couple):
            cross_spec = cross_block(couple[0], couple[1])
            lagged = jnp.dot(cross_spec.reshape(BLOCK * BLOCK, 2 * F), full_table, preferred_element_type=jnp.float32)
            return lagged.reshape(BLOCK, BLOCK, LAGS)
        lagged_all = lax.map(one_couple, (blocks, partner))
        results.append(lagged_all.reshape(NCH, BLOCK, LAGS))
    return jnp.stack(results, 0)
```

```python
import math

import jax
import jax.numpy as jnp
from jax import lax
from jax.experimental import pallas as pl
from jax.experimental.pallas import tpu as pltpu
from jax.sharding import PartitionSpec as P

F = 512
W = 64
LAGS = 128
ROUNDS = 3
BLOCK = 128
EPSILON = 1e-06

N_BLK = 32
RING = 4
CHUNKS = 4
ROWS = 32
BINS = 128
DEPTH = 128

F_UNROLL = 16
D_UNROLL = 8
C_UNROLL = 8

MESH = pl.DeviceIdType.MESH

STEPS = [
    (1, 0), (1, 1), (3, 0), (1, 2), (3, 1), (1, 3), (3, 2),
    (2, 0), (2, 1), (2, 2), (3, 3), (2, 3),
]
PASS_ON = {0: [0], 1: [1], 3: [2], 5: [3]}
SEND_SLOTS = 3
SUM_SLOTS = 4
LATE = 3


def lag_table(first_bin, bin_count, length_all, lag_count):
    bins = first_bin + jnp.arange(bin_count, dtype=jnp.int32)
    delays = jnp.arange(lag_count, dtype=jnp.int32) - lag_count // 2
    residue = jnp.mod(bins[:, None] * delays[None, :], 2 * length_all)
    phases = residue.astype(jnp.float32) * (math.pi / length_all)
    factor = 1.0 / math.sqrt(length_all)
    return jnp.stack([jnp.cos(phases) * factor, -jnp.sin(phases) * factor], 0).astype(jnp.bfloat16)


def normalize_chunk(spectra, live, turned, block, chunk):
    def channels(i, _):
        for u in range(C_UNROLL):
            row = i * C_UNROLL + u
            channel = chunk * ROWS + row
            values = spectra[:, channel].reshape(DEPTH, BINS).astype(jnp.float32)
            energy = jnp.sum(values * values, axis=0, keepdims=True) * (1.0 / DEPTH)
            weight = lax.rsqrt(energy + EPSILON) * live[channel].astype(jnp.float32)
            normed = (values * weight).astype(jnp.bfloat16).astype(jnp.float32)
            turned[pl.ds(row, BINS, stride=ROWS), :] = normed.T
        return 0

    lax.fori_loop(0, ROWS // C_UNROLL, channels, 0)

    def bins(i, _):
        for u in range(8):
            f = i * 8 + u
            rows = pl.ds(pl.multiple_of(f * ROWS, ROWS), ROWS)
            block[chunk, f] = turned[rows, :].astype(jnp.bfloat16)
        return 0

    lax.fori_loop(0, BINS // 8, bins, 0)


def cross_chunk(own, partner, cross, order):
    sign = jnp.where(lax.broadcasted_iota(jnp.int32, (ROWS, DEPTH), 1) < W, -1.0, 1.0)

    def bins(i, _):
        for u in range(F_UNROLL):
            f = i * F_UNROLL + u
            there = partner[f]
            swapped = (pltpu.roll(there.astype(jnp.float32), W, axis=1) * sign).astype(jnp.bfloat16)
            both = jnp.concatenate([there, swapped], axis=0)
            here = jnp.concatenate([own[o, f] for o in order], axis=0)
            parts = lax.dot_general(
                both, here, (((1,), (1,)), ((), ())), preferred_element_type=jnp.float32
            )
            cross[pl.ds(f, ROWS, stride=2 * BINS), :] = parts[:ROWS]
            cross[pl.ds(BINS + f, ROWS, stride=2 * BINS), :] = parts[ROWS:]
        return 0

    lax.fori_loop(0, BINS // F_UNROLL, bins, 0)


def lag_chunk(cross, table, keep, give):
    def channels(i, _):
        for u in range(D_UNROLL):
            j = i * D_UNROLL + u
            rows = pl.ds(pl.multiple_of(j * 2 * BINS, 2 * BINS), 2 * BINS)
            lags = lax.dot_general(
                cross[rows, :].astype(jnp.bfloat16),
                table[...],
                (((0,), (0,)), ((), ())),
                preferred_element_type=jnp.float32,
            )
            keep[0, j] = lags[:ROWS]
            keep[1, j] = lags[ROWS:2 * ROWS]
            give[0, j] = lags[2 * ROWS:3 * ROWS].astype(jnp.bfloat16)
            give[1, j] = lags[3 * ROWS:].astype(jnp.bfloat16)
        return 0

    lax.fori_loop(0, ROWS // D_UNROLL, channels, 0)


def kernel(
    spectra, live, table, out,
    first, second, third, passing, turned, cross, keep, total,
    core_out, core_in, pair_out, pair_in,
    down_send, up_send, far_send, second_recv, third_recv, far_recv,
    core_send, core_recv, pair_send, pair_recv,
):
    b = lax.axis_index("blk")
    q = lax.axis_index("frq")
    y = b % RING
    ring = b - y
    core = q + 1 - 2 * (q % 2)
    pair = (q + 2) % 4
    both = (core + 2) % 4
    order = [q, pair, core, both]
    below = (ring + (y + RING - 1) % RING, q)
    above = (ring + (y + 1) % RING, q)
    far_to = ((b + N_BLK - RING) % N_BLK, q)
    far_from = ((b + RING) % N_BLK, q)
    after = (b + 1) % N_BLK
    before = (b + N_BLK - 1) % N_BLK

    barrier = pltpu.get_barrier_semaphore()
    greeted = [
        below, above, far_to, far_from, (b, core), (b, pair),
        (after, q), (after, pair), (before, q), (before, pair),
    ]
    for device in greeted:
        pl.semaphore_signal(barrier, inc=1, device_id=device, device_id_type=MESH)

    def remote(src, dst, send, recv, device):
        return pltpu.make_async_remote_copy(
            src_ref=src, dst_ref=dst, send_sem=send, recv_sem=recv,
            device_id=device, device_id_type=MESH,
        )

    def down(src, c):
        return remote(src.at[c], second.at[c], down_send.at[c], second_recv.at[c], below)

    def up(src, c):
        return remote(src.at[c], third.at[c], up_send.at[c], third_recv.at[c], above)

    def far(c):
        return remote(first.at[c], passing.at[c], far_send.at[c], far_recv.at[c], far_to)

    for c in range(CHUNKS):
        normalize_chunk(spectra, live, turned, first, c)
        if c == 0:
            pl.semaphore_wait(barrier, len(greeted))

        @pl.when(y < RING - 1)
        def _():
            far(c).start()

        @pl.when(y > 0)
        def _():
            down(first, c).start()

        @pl.when(y == RING - 1)
        def _():
            up(first, c).start()

    def pass_on(c):
        @pl.when(y < RING - 1)
        def _():
            far(c).wait_recv()
            up(passing, c).start()

        @pl.when(y == 0)
        def _():
            down(passing, c).start()

    def core_copy(s):
        slot = s % SEND_SLOTS
        return remote(core_out.at[slot], core_in.at[s], core_send.at[s], core_recv.at[s], (b, core))

    def pair_copies(s):
        r, c = STEPS[s]
        slot = s % SUM_SLOTS
        if r == 2:
            a, z = 8 + c, 12 + c
            return [
                remote(pair_out.at[slot, 0], pair_in.at[a], pair_send.at[a], pair_recv.at[a], (after, q)),
                remote(pair_out.at[slot, 1], pair_in.at[z], pair_send.at[z], pair_recv.at[z], (after, pair)),
            ]
        a = (r // 2) * 4 + c
        return [remote(pair_out.at[slot, 1], pair_in.at[a], pair_send.at[a], pair_recv.at[a], (b, pair))]

    def add_cores(s):
        r, c = STEPS[s]
        core_copy(s).wait_recv()
        if s >= SUM_SLOTS:
            for copy in pair_copies(s - SUM_SLOTS):
                copy.wait_send()
        mine = keep[s % 2, 0] + core_in[s, 0].astype(jnp.float32)
        theirs = keep[s % 2, 1] + core_in[s, 1].astype(jnp.float32)
        slot = s % SUM_SLOTS
        pair_out[slot, 1] = theirs.astype(jnp.bfloat16)
        if r == 2:
            pair_out[slot, 0] = mine.astype(jnp.bfloat16)
        else:
            total[slot] = mine
        for copy in pair_copies(s):
            copy.start()

    def finish(s):
        r, c = STEPS[s]
        for copy in pair_copies(s):
            copy.wait_recv()
        if r == 2:
            lags = pair_in[8 + c].astype(jnp.float32) + pair_in[12 + c].astype(jnp.float32)
        else:
            lags = total[s % SUM_SLOTS] + pair_in[(r // 2) * 4 + c].astype(jnp.float32)
        out[r - 1, c] = lags

    for s, (r, c) in enumerate(STEPS):
        for p in PASS_ON.get(s, []):
            pass_on(p)
        if r == 1:
            down(first, c).wait_recv()
        if r == 3:
            up(first, c).wait_recv()
        here = second if r == 2 else first
        there = second if r == 1 else third
        cross_chunk(here, there.at[c], cross, order)
        if s >= SEND_SLOTS:
            core_copy(s - SEND_SLOTS).wait_send()
        lag_chunk(cross, table, keep.at[s % 2], core_out.at[s % SEND_SLOTS])
        core_copy(s).start()
        if s >= 1:
            add_cores(s - 1)
        if s >= LATE:
            finish(s - LATE)
    last = len(STEPS)
    add_cores(last - 1)
    for s in range(last - LATE, last):
        finish(s)

    for c in range(CHUNKS):
        down(first, c).wait_send()
        up(first, c).wait_send()

        @pl.when(y < RING - 1)
        def _():
            far(c).wait_send()

    for s in range(last - SEND_SLOTS, last):
        core_copy(s).wait_send()
    for s in range(last - SUM_SLOTS, last):
        for copy in pair_copies(s):
            copy.wait_send()


def local(spectra, live):
    table = lag_table(lax.axis_index("frq") * BINS, BINS, F, LAGS)
    table = (table * (1.0 / math.sqrt(W))).reshape(2 * BINS, LAGS)
    block = (CHUNKS, BINS, ROWS, DEPTH)
    piece = (ROWS, ROWS, LAGS)
    half = jnp.bfloat16
    lags = pl.pallas_call(
        kernel,
        out_shape=jax.ShapeDtypeStruct((ROUNDS, CHUNKS) + piece, jnp.float32),
        in_specs=[
            pl.BlockSpec(memory_space=pltpu.VMEM),
            pl.BlockSpec(memory_space=pltpu.SMEM),
            pl.BlockSpec(memory_space=pltpu.VMEM),
        ],
        out_specs=pl.BlockSpec(memory_space=pltpu.VMEM),
        scratch_shapes=[
            pltpu.VMEM(block, half),
            pltpu.VMEM(block, half),
            pltpu.VMEM(block, half),
            pltpu.VMEM(block, half),
            pltpu.VMEM((BINS * ROWS, DEPTH), jnp.float32),
            pltpu.VMEM((ROWS * 2 * BINS, BLOCK), jnp.float32),
            pltpu.VMEM((2, 2) + piece, jnp.float32),
            pltpu.VMEM((SUM_SLOTS,) + piece, jnp.float32),
            pltpu.VMEM((SEND_SLOTS, 2) + piece, half),
            pltpu.VMEM((len(STEPS), 2) + piece, half),
            pltpu.VMEM((SUM_SLOTS, 2) + piece, half),
            pltpu.VMEM((16,) + piece, half),
            pltpu.SemaphoreType.DMA((CHUNKS,)),
            pltpu.SemaphoreType.DMA((CHUNKS,)),
            pltpu.SemaphoreType.DMA((CHUNKS,)),
            pltpu.SemaphoreType.DMA((CHUNKS,)),
            pltpu.SemaphoreType.DMA((CHUNKS,)),
            pltpu.SemaphoreType.DMA((CHUNKS,)),
            pltpu.SemaphoreType.DMA((len(STEPS),)),
            pltpu.SemaphoreType.DMA((len(STEPS),)),
            pltpu.SemaphoreType.DMA((16,)),
            pltpu.SemaphoreType.DMA((16,)),
        ],
        compiler_params=pltpu.CompilerParams(
            collective_id=0, has_side_effects=True, vmem_limit_bytes=60 * 2**20
        ),
    )(spectra, live, table)
    return lags.reshape(ROUNDS, BLOCK, ROWS, LAGS).transpose(0, 2, 1, 3)


def solution(mesh):
    return jax.shard_map(
        local,
        mesh=mesh,
        in_specs=(P(None, "blk", None, "frq"), P("blk")),
        out_specs=P(None, ("blk", "frq"), None, None),
        check_vma=False,
    )
```

```python
import math

import jax
import jax.numpy as jnp
from jax import lax
from jax.experimental import pallas as pl
from jax.experimental.pallas import tpu as pltpu
from jax.sharding import PartitionSpec as P

F = 512
W = 64
LAGS = 128
ROUNDS = 3
BLOCK = 128
EPSILON = 1e-06

N_BLK = 32
RING = 4
CHUNKS = 4
ROWS = 32
BINS = 128
DEPTH = 128

F_UNROLL = 32
D_UNROLL = 16
C_UNROLL = 8

MESH = pl.DeviceIdType.MESH

STEPS = [
    (1, 0), (1, 1), (3, 0), (1, 2), (3, 1), (1, 3), (3, 2),
    (2, 0), (2, 1), (2, 2), (3, 3), (2, 3),
]
PASS_ON = {0: [0], 1: [1], 3: [2], 5: [3]}
SEND_SLOTS = 3
RELEASE = 5
FINISH = {8: [0, 1], 9: [2, 3], 10: [4, 5], 11: [6, 7]}


def lag_table(first_bin, bin_count, length_all, lag_count):
    bins = first_bin + jnp.arange(bin_count, dtype=jnp.int32)
    delays = jnp.arange(lag_count, dtype=jnp.int32) - lag_count // 2
    residue = jnp.mod(bins[:, None] * delays[None, :], 2 * length_all)
    phases = residue.astype(jnp.float32) * (math.pi / length_all)
    factor = 1.0 / math.sqrt(length_all)
    return jnp.stack([jnp.cos(phases) * factor, -jnp.sin(phases) * factor], 0).astype(jnp.bfloat16)


def normalize_chunk(spectra, live, turned, block, chunk):
    def channels(i, _):
        for u in range(C_UNROLL):
            row = i * C_UNROLL + u
            channel = chunk * ROWS + row
            values = spectra[:, channel].reshape(DEPTH, BINS).astype(jnp.float32)
            energy = jnp.sum(values * values, axis=0, keepdims=True) * (1.0 / DEPTH)
            weight = lax.rsqrt(energy + EPSILON) * live[channel].astype(jnp.float32)
            normed = (values * weight).astype(jnp.bfloat16).astype(jnp.float32)
            turned[pl.ds(row, BINS, stride=ROWS), :] = normed.T
        return 0

    lax.fori_loop(0, ROWS // C_UNROLL, channels, 0)

    def bins(i, _):
        for u in range(8):
            f = i * 8 + u
            rows = pl.ds(pl.multiple_of(f * ROWS, ROWS), ROWS)
            block[chunk, f] = turned[rows, :].astype(jnp.bfloat16)
        return 0

    lax.fori_loop(0, BINS // 8, bins, 0)


def cross_chunk(own, partner, cross, order):
    sign = jnp.where(lax.broadcasted_iota(jnp.int32, (ROWS, DEPTH), 1) < W, -1.0, 1.0)

    def bins(i, _):
        for u in range(F_UNROLL):
            f = i * F_UNROLL + u
            there = partner[f]
            swapped = (pltpu.roll(there.astype(jnp.float32), W, axis=1) * sign).astype(jnp.bfloat16)
            both = jnp.concatenate([there, swapped], axis=0)
            here = jnp.concatenate([own[o, f] for o in order], axis=0)
            parts = lax.dot_general(
                both, here, (((1,), (1,)), ((), ())), preferred_element_type=jnp.float32
            )
            cross[pl.ds(f, ROWS, stride=2 * BINS), :] = parts[:ROWS]
            cross[pl.ds(BINS + f, ROWS, stride=2 * BINS), :] = parts[ROWS:]
        return 0

    lax.fori_loop(0, BINS // F_UNROLL, bins, 0)


def lag_chunk(cross, table, keep, give):
    def channels(i, _):
        for u in range(D_UNROLL):
            j = i * D_UNROLL + u
            rows = pl.ds(pl.multiple_of(j * 2 * BINS, 2 * BINS), 2 * BINS)
            lags = lax.dot_general(
                cross[rows, :].astype(jnp.bfloat16),
                table[...],
                (((0,), (0,)), ((), ())),
                preferred_element_type=jnp.float32,
            )
            keep[0, j] = lags[:ROWS]
            keep[1, j] = lags[ROWS:2 * ROWS]
            give[0, j] = lags[2 * ROWS:3 * ROWS].astype(jnp.bfloat16)
            give[1, j] = lags[3 * ROWS:].astype(jnp.bfloat16)
        return 0

    lax.fori_loop(0, ROWS // D_UNROLL, channels, 0)


def kernel(
    spectra, live, table, out,
    first, second, third, passing, turned, cross, keep, total,
    core_out, core_in, pair_out, pair_in,
    down_send, up_send, far_send, second_recv, third_recv, far_recv,
    core_send, core_recv, pair_send, pair_recv,
):
    b = lax.axis_index("blk")
    q = lax.axis_index("frq")
    y = b % RING
    ring = b - y
    core = q + 1 - 2 * (q % 2)
    pair = (q + 2) % 4
    both = (core + 2) % 4
    order = [q, pair, core, both]
    below = (ring + (y + RING - 1) % RING, q)
    above = (ring + (y + 1) % RING, q)
    far_to = ((b + N_BLK - RING) % N_BLK, q)
    far_from = ((b + RING) % N_BLK, q)
    after = (b + 1) % N_BLK
    before = (b + N_BLK - 1) % N_BLK

    barrier = pltpu.get_barrier_semaphore()
    greeted = [
        below, above, far_to, far_from, (b, core), (b, pair),
        (after, q), (after, pair), (before, q), (before, pair),
    ]
    for device in greeted:
        pl.semaphore_signal(barrier, inc=1, device_id=device, device_id_type=MESH)

    def remote(src, dst, send, recv, device):
        return pltpu.make_async_remote_copy(
            src_ref=src, dst_ref=dst, send_sem=send, recv_sem=recv,
            device_id=device, device_id_type=MESH,
        )

    def down(src, c):
        return remote(src.at[c], second.at[c], down_send.at[c], second_recv.at[c], below)

    def up(src, c):
        return remote(src.at[c], third.at[c], up_send.at[c], third_recv.at[c], above)

    def far(c):
        return remote(first.at[c], passing.at[c], far_send.at[c], far_recv.at[c], far_to)

    for c in range(CHUNKS):
        normalize_chunk(spectra, live, turned, first, c)
        if c == 0:
            pl.semaphore_wait(barrier, len(greeted))

        @pl.when(y < RING - 1)
        def _():
            far(c).start()

        @pl.when(y > 0)
        def _():
            down(first, c).start()

        @pl.when(y == RING - 1)
        def _():
            up(first, c).start()

    def pass_on(c):
        @pl.when(y < RING - 1)
        def _():
            far(c).wait_recv()
            up(passing, c).start()

        @pl.when(y == 0)
        def _():
            down(passing, c).start()

    def core_copy(s):
        slot = s % SEND_SLOTS
        return remote(core_out.at[slot], core_in.at[s], core_send.at[s], core_recv.at[s], (b, core))

    def pair_copies(s):
        r, c = STEPS[s]
        slot = s
        if r == 2:
            a, z = 8 + c, 12 + c
            return [
                remote(pair_out.at[slot, 0], pair_in.at[a], pair_send.at[a], pair_recv.at[a], (after, q)),
                remote(pair_out.at[slot, 1], pair_in.at[z], pair_send.at[z], pair_recv.at[z], (after, pair)),
            ]
        a = (r // 2) * 4 + c
        return [remote(pair_out.at[slot, 1], pair_in.at[a], pair_send.at[a], pair_recv.at[a], (b, pair))]

    def add_cores(s):
        r, c = STEPS[s]
        core_copy(s).wait_recv()
        mine = keep[s % 2, 0] + core_in[s, 0].astype(jnp.float32)
        theirs = keep[s % 2, 1] + core_in[s, 1].astype(jnp.float32)
        pair_out[s, 1] = theirs.astype(jnp.bfloat16)
        if r == 2:
            pair_out[s, 0] = mine.astype(jnp.bfloat16)
        else:
            total[(r // 2) * 4 + c] = mine

    def exchange(s):
        for copy in pair_copies(s):
            copy.start()

    def finish(s):
        r, c = STEPS[s]
        for copy in pair_copies(s):
            copy.wait_recv()
        if r == 2:
            lags = pair_in[8 + c].astype(jnp.float32) + pair_in[12 + c].astype(jnp.float32)
        else:
            lags = total[(r // 2) * 4 + c] + pair_in[(r // 2) * 4 + c].astype(jnp.float32)
        out[r - 1, c] = lags

    for s, (r, c) in enumerate(STEPS):
        for p in PASS_ON.get(s, []):
            pass_on(p)
        if s == RELEASE:
            for held in range(s - 1):
                exchange(held)
        if r == 1:
            down(first, c).wait_recv()
        if r == 3:
            up(first, c).wait_recv()
        here = second if r == 2 else first
        there = second if r == 1 else third
        cross_chunk(here, there.at[c], cross, order)
        if s >= SEND_SLOTS:
            core_copy(s - SEND_SLOTS).wait_send()
        lag_chunk(cross, table, keep.at[s % 2], core_out.at[s % SEND_SLOTS])
        core_copy(s).start()
        if s >= 1:
            add_cores(s - 1)
        if s >= RELEASE:
            exchange(s - 1)
        for done in FINISH.get(s, []):
            finish(done)
    last = len(STEPS)
    add_cores(last - 1)
    exchange(last - 1)
    for s in range(FINISH[last - 1][-1] + 1, last):
        finish(s)

    for c in range(CHUNKS):
        down(first, c).wait_send()
        up(first, c).wait_send()

        @pl.when(y < RING - 1)
        def _():
            far(c).wait_send()

    for s in range(last - SEND_SLOTS, last):
        core_copy(s).wait_send()
    for s in range(last):
        for copy in pair_copies(s):
            copy.wait_send()


def local(spectra, live):
    table = lag_table(lax.axis_index("frq") * BINS, BINS, F, LAGS)
    table = (table * (1.0 / math.sqrt(W))).reshape(2 * BINS, LAGS)
    block = (CHUNKS, BINS, ROWS, DEPTH)
    piece = (ROWS, ROWS, LAGS)
    half = jnp.bfloat16
    lags = pl.pallas_call(
        kernel,
        out_shape=jax.ShapeDtypeStruct((ROUNDS, CHUNKS) + piece, jnp.float32),
        in_specs=[
            pl.BlockSpec(memory_space=pltpu.VMEM),
            pl.BlockSpec(memory_space=pltpu.SMEM),
            pl.BlockSpec(memory_space=pltpu.VMEM),
        ],
        out_specs=pl.BlockSpec(memory_space=pltpu.VMEM),
        scratch_shapes=[
            pltpu.VMEM(block, half),
            pltpu.VMEM(block, half),
            pltpu.VMEM(block, half),
            pltpu.VMEM(block, half),
            pltpu.VMEM((BINS * ROWS, DEPTH), jnp.float32),
            pltpu.VMEM((ROWS * 2 * BINS, BLOCK), jnp.float32),
            pltpu.VMEM((2, 2) + piece, jnp.float32),
            pltpu.VMEM((2 * CHUNKS,) + piece, jnp.float32),
            pltpu.VMEM((SEND_SLOTS, 2) + piece, half),
            pltpu.VMEM((len(STEPS), 2) + piece, half),
            pltpu.VMEM((len(STEPS), 2) + piece, half),
            pltpu.VMEM((16,) + piece, half),
            pltpu.SemaphoreType.DMA((CHUNKS,)),
            pltpu.SemaphoreType.DMA((CHUNKS,)),
            pltpu.SemaphoreType.DMA((CHUNKS,)),
            pltpu.SemaphoreType.DMA((CHUNKS,)),
            pltpu.SemaphoreType.DMA((CHUNKS,)),
            pltpu.SemaphoreType.DMA((CHUNKS,)),
            pltpu.SemaphoreType.DMA((len(STEPS),)),
            pltpu.SemaphoreType.DMA((len(STEPS),)),
            pltpu.SemaphoreType.DMA((16,)),
            pltpu.SemaphoreType.DMA((16,)),
        ],
        compiler_params=pltpu.CompilerParams(
            collective_id=0, has_side_effects=True, vmem_limit_bytes=60 * 2**20
        ),
    )(spectra, live, table)
    return lags.reshape(ROUNDS, BLOCK, ROWS, LAGS).transpose(0, 2, 1, 3)


def solution(mesh):
    return jax.shard_map(
        local,
        mesh=mesh,
        in_specs=(P(None, "blk", None, "frq"), P("blk")),
        out_specs=P(None, ("blk", "frq"), None, None),
        check_vma=False,
    )
```

```python
import math

import jax
import jax.numpy as jnp
from jax import lax
from jax.experimental import pallas as pl
from jax.experimental.pallas import tpu as pltpu
from jax.sharding import PartitionSpec as P

F = 512
W = 64
LAGS = 128
ROUNDS = 3
BLOCK = 128
EPSILON = 1e-06

N_BLK = 32
RING = 4
CHUNKS = 4
ROWS = 32
BINS = 128
DEPTH = 128

F_UNROLL = 32
D_UNROLL = 16
C_UNROLL = 8

MESH = pl.DeviceIdType.MESH

STEPS = [
    (1, 0), (1, 1), (3, 0), (1, 2), (3, 1), (1, 3),
    (2, 0), (2, 1), (3, 2), (2, 2), (3, 3), (2, 3),
]
GROUPS = [[0], [1], [2], [3], [4], [5], [6, 7], [8, 9], [10, 11]]
PASS_ON = {0: [0], 1: [1], 3: [2], 5: [3]}
SEND_SLOTS = 3
RELEASE = 5
FINISH = {8: [0, 1], 9: [2, 3], 10: [4, 5], 11: [6, 7]}


def lag_table(first_bin, bin_count, length_all, lag_count):
    bins = first_bin + jnp.arange(bin_count, dtype=jnp.int32)
    delays = jnp.arange(lag_count, dtype=jnp.int32) - lag_count // 2
    residue = jnp.mod(bins[:, None] * delays[None, :], 2 * length_all)
    phases = residue.astype(jnp.float32) * (math.pi / length_all)
    factor = 1.0 / math.sqrt(length_all)
    return jnp.stack([jnp.cos(phases) * factor, -jnp.sin(phases) * factor], 0).astype(jnp.bfloat16)


def normalize_chunk(spectra, live, turned, block, chunk):
    def channels(i, _):
        for u in range(C_UNROLL):
            row = i * C_UNROLL + u
            channel = chunk * ROWS + row
            values = spectra[:, channel].reshape(DEPTH, BINS).astype(jnp.float32)
            energy = jnp.sum(values * values, axis=0, keepdims=True) * (1.0 / DEPTH)
            weight = lax.rsqrt(energy + EPSILON) * live[channel].astype(jnp.float32)
            normed = (values * weight).astype(jnp.bfloat16).astype(jnp.float32)
            turned[pl.ds(row, BINS, stride=ROWS), :] = normed.T
        return 0

    lax.fori_loop(0, ROWS // C_UNROLL, channels, 0)

    def bins(i, _):
        for u in range(8):
            f = i * 8 + u
            rows = pl.ds(pl.multiple_of(f * ROWS, ROWS), ROWS)
            block[chunk, f] = turned[rows, :].astype(jnp.bfloat16)
        return 0

    lax.fori_loop(0, BINS // 8, bins, 0)


def cross_chunk(owns, partners, crosses, order):
    sign = jnp.where(lax.broadcasted_iota(jnp.int32, (ROWS, DEPTH), 1) < W, -1.0, 1.0)

    def bins(i, _):
        for u in range(F_UNROLL):
            f = i * F_UNROLL + u
            both = []
            for partner in partners:
                there = partner[f]
                swapped = pltpu.roll(there.astype(jnp.float32), W, axis=1) * sign
                both += [there, swapped.astype(jnp.bfloat16)]
            here = jnp.concatenate([own[o, f] for own in owns for o in order], axis=0)
            parts = lax.dot_general(
                jnp.concatenate(both, axis=0),
                here,
                (((1,), (1,)), ((), ())),
                preferred_element_type=jnp.float32,
            )
            for k, cross in enumerate(crosses):
                row, column = (2 * ROWS * k, 0) if len(partners) > 1 else (0, BLOCK * k)
                columns = slice(column, column + BLOCK)
                cross[pl.ds(f, ROWS, stride=2 * BINS), :] = parts[row:row + ROWS, columns]
                cross[pl.ds(BINS + f, ROWS, stride=2 * BINS), :] = parts[row + ROWS:row + 2 * ROWS, columns]
        return 0

    lax.fori_loop(0, BINS // F_UNROLL, bins, 0)


def lag_chunk(cross, table, keep, give):
    def channels(i, _):
        for u in range(D_UNROLL):
            j = i * D_UNROLL + u
            rows = pl.ds(pl.multiple_of(j * 2 * BINS, 2 * BINS), 2 * BINS)
            lags = lax.dot_general(
                cross[rows, :].astype(jnp.bfloat16),
                table[...],
                (((0,), (0,)), ((), ())),
                preferred_element_type=jnp.float32,
            )
            keep[0, j] = lags[:ROWS]
            keep[1, j] = lags[ROWS:2 * ROWS]
            give[0, j] = lags[2 * ROWS:3 * ROWS].astype(jnp.bfloat16)
            give[1, j] = lags[3 * ROWS:].astype(jnp.bfloat16)
        return 0

    lax.fori_loop(0, ROWS // D_UNROLL, channels, 0)


def kernel(
    spectra, live, table, out,
    first, second, third, passing, cross, cross_too, keep, total,
    core_out, core_in, pair_out, pair_in,
    down_send, up_send, far_send, second_recv, third_recv, far_recv,
    core_send, core_recv, pair_send, pair_recv,
):
    b = lax.axis_index("blk")
    q = lax.axis_index("frq")
    y = b % RING
    ring = b - y
    core = q + 1 - 2 * (q % 2)
    pair = (q + 2) % 4
    both = (core + 2) % 4
    order = [q, pair, core, both]
    below = (ring + (y + RING - 1) % RING, q)
    above = (ring + (y + 1) % RING, q)
    far_to = ((b + N_BLK - RING) % N_BLK, q)
    far_from = ((b + RING) % N_BLK, q)
    after = (b + 1) % N_BLK
    before = (b + N_BLK - 1) % N_BLK

    barrier = pltpu.get_barrier_semaphore()
    greeted = [
        below, above, far_to, far_from, (b, core), (b, pair),
        (after, q), (after, pair), (before, q), (before, pair),
    ]
    for device in greeted:
        pl.semaphore_signal(barrier, inc=1, device_id=device, device_id_type=MESH)

    def remote(src, dst, send, recv, device):
        return pltpu.make_async_remote_copy(
            src_ref=src, dst_ref=dst, send_sem=send, recv_sem=recv,
            device_id=device, device_id_type=MESH,
        )

    def down(src, c):
        return remote(src.at[c], second.at[c], down_send.at[c], second_recv.at[c], below)

    def up(src, c):
        return remote(src.at[c], third.at[c], up_send.at[c], third_recv.at[c], above)

    def far(c):
        return remote(first.at[c], passing.at[c], far_send.at[c], far_recv.at[c], far_to)

    for c in range(CHUNKS):
        normalize_chunk(spectra, live, cross, first, c)
        if c == 0:
            pl.semaphore_wait(barrier, len(greeted))

        @pl.when(y < RING - 1)
        def _():
            far(c).start()

        @pl.when(y > 0)
        def _():
            down(first, c).start()

        @pl.when(y == RING - 1)
        def _():
            up(first, c).start()

    def pass_on(c):
        @pl.when(y < RING - 1)
        def _():
            far(c).wait_recv()
            up(passing, c).start()

        @pl.when(y == 0)
        def _():
            down(passing, c).start()

    def core_copy(s):
        slot = s % SEND_SLOTS
        return remote(core_out.at[slot], core_in.at[s], core_send.at[s], core_recv.at[s], (b, core))

    def pair_copies(s):
        r, c = STEPS[s]
        slot = s
        if r == 2:
            a, z = 8 + c, 12 + c
            return [
                remote(pair_out.at[slot, 0], pair_in.at[a], pair_send.at[a], pair_recv.at[a], (after, q)),
                remote(pair_out.at[slot, 1], pair_in.at[z], pair_send.at[z], pair_recv.at[z], (after, pair)),
            ]
        a = (r // 2) * 4 + c
        return [remote(pair_out.at[slot, 1], pair_in.at[a], pair_send.at[a], pair_recv.at[a], (b, pair))]

    def add_cores(s):
        r, c = STEPS[s]
        core_copy(s).wait_recv()
        mine = keep[s % 2, 0] + core_in[s, 0].astype(jnp.float32)
        theirs = keep[s % 2, 1] + core_in[s, 1].astype(jnp.float32)
        pair_out[s, 1] = theirs.astype(jnp.bfloat16)
        if r == 2:
            pair_out[s, 0] = mine.astype(jnp.bfloat16)
        else:
            total[(r // 2) * 4 + c] = mine

    def exchange(s):
        for copy in pair_copies(s):
            copy.start()

    def finish(s):
        r, c = STEPS[s]
        for copy in pair_copies(s):
            copy.wait_recv()
        if r == 2:
            lags = pair_in[8 + c].astype(jnp.float32) + pair_in[12 + c].astype(jnp.float32)
        else:
            lags = total[(r // 2) * 4 + c] + pair_in[(r // 2) * 4 + c].astype(jnp.float32)
        out[r - 1, c] = lags

    def prepare(s):
        r, c = STEPS[s]
        for p in PASS_ON.get(s, []):
            pass_on(p)
        if s == RELEASE:
            for held in range(s - 1):
                exchange(held)
        if r == 1:
            down(first, c).wait_recv()
        if r == 3:
            up(first, c).wait_recv()

    def after_cross(s, cross):
        if s >= SEND_SLOTS:
            core_copy(s - SEND_SLOTS).wait_send()
        lag_chunk(cross, table, keep.at[s % 2], core_out.at[s % SEND_SLOTS])
        core_copy(s).start()
        if s >= 1:
            add_cores(s - 1)
        if s >= RELEASE:
            exchange(s - 1)
        for done in FINISH.get(s, []):
            finish(done)

    for group in GROUPS:
        for s in group:
            prepare(s)
        owns, partners = [], []
        for s in group:
            r, c = STEPS[s]
            own = (r == 2, second if r == 2 else first)
            partner = (r == 1, c, (second if r == 1 else third).at[c])
            if own[0] not in [o[0] for o in owns]:
                owns.append(own)
            if partner[:2] not in [p[:2] for p in partners]:
                partners.append(partner)
        crosses = [cross, cross_too][:len(group)]
        cross_chunk([o[-1] for o in owns], [p[-1] for p in partners], crosses, order)
        for s, done in zip(group, crosses):
            after_cross(s, done)
    last = len(STEPS)
    add_cores(last - 1)
    exchange(last - 1)
    for s in range(FINISH[last - 1][-1] + 1, last):
        finish(s)

    for c in range(CHUNKS):
        down(first, c).wait_send()
        up(first, c).wait_send()

        @pl.when(y < RING - 1)
        def _():
            far(c).wait_send()

    for s in range(last - SEND_SLOTS, last):
        core_copy(s).wait_send()
    for s in range(last):
        for copy in pair_copies(s):
            copy.wait_send()


def local(spectra, live):
    table = lag_table(lax.axis_index("frq") * BINS, BINS, F, LAGS)
    table = (table * (1.0 / math.sqrt(W))).reshape(2 * BINS, LAGS)
    block = (CHUNKS, BINS, ROWS, DEPTH)
    piece = (ROWS, ROWS, LAGS)
    half = jnp.bfloat16
    lags = pl.pallas_call(
        kernel,
        out_shape=jax.ShapeDtypeStruct((ROUNDS, CHUNKS) + piece, jnp.float32),
        in_specs=[
            pl.BlockSpec(memory_space=pltpu.VMEM),
            pl.BlockSpec(memory_space=pltpu.SMEM),
            pl.BlockSpec(memory_space=pltpu.VMEM),
        ],
        out_specs=pl.BlockSpec(memory_space=pltpu.VMEM),
        scratch_shapes=[
            pltpu.VMEM(block, half),
            pltpu.VMEM(block, half),
            pltpu.VMEM(block, half),
            pltpu.VMEM(block, half),
            pltpu.VMEM((ROWS * 2 * BINS, BLOCK), jnp.float32),
            pltpu.VMEM((ROWS * 2 * BINS, BLOCK), jnp.float32),
            pltpu.VMEM((2, 2) + piece, jnp.float32),
            pltpu.VMEM((2 * CHUNKS,) + piece, jnp.float32),
            pltpu.VMEM((SEND_SLOTS, 2) + piece, half),
            pltpu.VMEM((len(STEPS), 2) + piece, half),
            pltpu.VMEM((len(STEPS), 2) + piece, half),
            pltpu.VMEM((16,) + piece, half),
            pltpu.SemaphoreType.DMA((CHUNKS,)),
            pltpu.SemaphoreType.DMA((CHUNKS,)),
            pltpu.SemaphoreType.DMA((CHUNKS,)),
            pltpu.SemaphoreType.DMA((CHUNKS,)),
            pltpu.SemaphoreType.DMA((CHUNKS,)),
            pltpu.SemaphoreType.DMA((CHUNKS,)),
            pltpu.SemaphoreType.DMA((len(STEPS),)),
            pltpu.SemaphoreType.DMA((len(STEPS),)),
            pltpu.SemaphoreType.DMA((16,)),
            pltpu.SemaphoreType.DMA((16,)),
        ],
        compiler_params=pltpu.CompilerParams(
            collective_id=0, has_side_effects=True, vmem_limit_bytes=60 * 2**20
        ),
    )(spectra, live, table)
    return lags.reshape(ROUNDS, BLOCK, ROWS, LAGS).transpose(0, 2, 1, 3)


def solution(mesh):
    return jax.shard_map(
        local,
        mesh=mesh,
        in_specs=(P(None, "blk", None, "frq"), P("blk")),
        out_specs=P(None, ("blk", "frq"), None, None),
        check_vma=False,
    )
```

```python
import math

import jax
import jax.numpy as jnp
from jax import lax
from jax.experimental import pallas as pl
from jax.experimental.pallas import tpu as pltpu
from jax.sharding import PartitionSpec as P

F = 512
W = 64
LAGS = 128
ROUNDS = 3
BLOCK = 128
EPSILON = 1e-06

N_BLK = 32
RING = 4
CHUNKS = 4
ROWS = 32
BINS = 128
DEPTH = 128

F_UNROLL = 32
D_UNROLL = 16
C_UNROLL = 8

MESH = pl.DeviceIdType.MESH

STEPS = [
    (1, 0), (1, 1), (3, 0), (1, 2), (3, 1), (1, 3),
    (2, 0), (2, 1), (3, 2), (2, 2), (3, 3), (2, 3),
]
GROUPS = [[0], [1], [2], [3], [4], [5], [6, 7], [8, 9], [10, 11]]
PASS_ON = {0: [0], 1: [1], 3: [2], 5: [3]}
SEND_SLOTS = 3
RELEASE = 5
FINISH = {8: [0, 1], 9: [2, 3], 10: [4, 5]}


def lag_table(first_bin, bin_count, length_all, lag_count):
    bins = first_bin + jnp.arange(bin_count, dtype=jnp.int32)
    delays = jnp.arange(lag_count, dtype=jnp.int32) - lag_count // 2
    residue = jnp.mod(bins[:, None] * delays[None, :], 2 * length_all)
    phases = residue.astype(jnp.float32) * (math.pi / length_all)
    factor = 1.0 / math.sqrt(length_all)
    return jnp.stack([jnp.cos(phases) * factor, -jnp.sin(phases) * factor], 0).astype(jnp.bfloat16)


def normalize_chunk(spectra, live, turned, block, chunk):
    def channels(i, _):
        for u in range(C_UNROLL):
            row = i * C_UNROLL + u
            channel = chunk * ROWS + row
            values = spectra[:, channel].reshape(DEPTH, BINS).astype(jnp.float32)
            energy = jnp.sum(values * values, axis=0, keepdims=True) * (1.0 / DEPTH)
            weight = lax.rsqrt(energy + EPSILON) * live[channel].astype(jnp.float32)
            normed = (values * weight).astype(jnp.bfloat16).astype(jnp.float32)
            turned[pl.ds(row, BINS, stride=ROWS), :] = normed.T
        return 0

    lax.fori_loop(0, ROWS // C_UNROLL, channels, 0)

    def bins(i, _):
        for u in range(8):
            f = i * 8 + u
            rows = pl.ds(pl.multiple_of(f * ROWS, ROWS), ROWS)
            block[chunk, f] = turned[rows, :].astype(jnp.bfloat16)
        return 0

    lax.fori_loop(0, BINS // 8, bins, 0)


def cross_chunk(owns, partners, crosses, order):
    sign = jnp.where(lax.broadcasted_iota(jnp.int32, (ROWS, DEPTH), 1) < W, -1.0, 1.0)

    def bins(i, _):
        for u in range(F_UNROLL):
            f = i * F_UNROLL + u
            both = []
            for partner in partners:
                there = partner[f]
                swapped = pltpu.roll(there.astype(jnp.float32), W, axis=1) * sign
                both += [there, swapped.astype(jnp.bfloat16)]
            here = jnp.concatenate([own[o, f] for own in owns for o in order], axis=0)
            parts = lax.dot_general(
                jnp.concatenate(both, axis=0),
                here,
                (((1,), (1,)), ((), ())),
                preferred_element_type=jnp.float32,
            )
            for k, cross in enumerate(crosses):
                row, column = (2 * ROWS * k, 0) if len(partners) > 1 else (0, BLOCK * k)
                columns = slice(column, column + BLOCK)
                cross[pl.ds(f, ROWS, stride=2 * BINS), :] = parts[row:row + ROWS, columns]
                cross[pl.ds(BINS + f, ROWS, stride=2 * BINS), :] = parts[row + ROWS:row + 2 * ROWS, columns]
        return 0

    lax.fori_loop(0, BINS // F_UNROLL, bins, 0)


def lag_chunk(cross, table, keep, give):
    def channels(i, _):
        for u in range(D_UNROLL):
            j = i * D_UNROLL + u
            rows = pl.ds(pl.multiple_of(j * 2 * BINS, 2 * BINS), 2 * BINS)
            lags = lax.dot_general(
                cross[rows, :].astype(jnp.bfloat16),
                table[...],
                (((0,), (0,)), ((), ())),
                preferred_element_type=jnp.float32,
            )
            keep[0, j] = lags[:ROWS]
            keep[1, j] = lags[ROWS:2 * ROWS]
            give[0, j] = lags[2 * ROWS:3 * ROWS].astype(jnp.bfloat16)
            give[1, j] = lags[3 * ROWS:].astype(jnp.bfloat16)
        return 0

    lax.fori_loop(0, ROWS // D_UNROLL, channels, 0)


def kernel(
    spectra, live, table, out,
    first, second, third, passing, cross, cross_too, keep, total,
    core_out, core_in, pair_out, pair_in,
    down_send, up_send, far_send, second_recv, third_recv, far_recv,
    core_send, core_recv, pair_send, pair_recv,
):
    b = lax.axis_index("blk")
    q = lax.axis_index("frq")
    y = b % RING
    ring = b - y
    core = q + 1 - 2 * (q % 2)
    pair = (q + 2) % 4
    both = (core + 2) % 4
    order = [q, pair, core, both]
    below = (ring + (y + RING - 1) % RING, q)
    above = (ring + (y + 1) % RING, q)
    far_to = ((b + N_BLK - RING) % N_BLK, q)
    far_from = ((b + RING) % N_BLK, q)
    after = (b + 1) % N_BLK
    before = (b + N_BLK - 1) % N_BLK

    barrier = pltpu.get_barrier_semaphore()
    greeted = [
        below, above, far_to, far_from, (b, core), (b, pair),
        (after, q), (after, pair), (before, q), (before, pair),
    ]
    for device in greeted:
        pl.semaphore_signal(barrier, inc=1, device_id=device, device_id_type=MESH)

    def remote(src, dst, send, recv, device):
        return pltpu.make_async_remote_copy(
            src_ref=src, dst_ref=dst, send_sem=send, recv_sem=recv,
            device_id=device, device_id_type=MESH,
        )

    def down(src, c):
        return remote(src.at[c], second.at[c], down_send.at[c], second_recv.at[c], below)

    def up(src, c):
        return remote(src.at[c], third.at[c], up_send.at[c], third_recv.at[c], above)

    def far(c):
        return remote(first.at[c], passing.at[c], far_send.at[c], far_recv.at[c], far_to)

    for c in range(CHUNKS):
        normalize_chunk(spectra, live, cross, first, c)
        if c == 0:
            pl.semaphore_wait(barrier, len(greeted))

        @pl.when(y < RING - 1)
        def _():
            far(c).start()

        @pl.when(y > 0)
        def _():
            down(first, c).start()

        @pl.when(y == RING - 1)
        def _():
            up(first, c).start()

    def pass_on(c):
        @pl.when(y < RING - 1)
        def _():
            far(c).wait_recv()
            up(passing, c).start()

        @pl.when(y == 0)
        def _():
            down(passing, c).start()

    def core_copy(s):
        slot = s % SEND_SLOTS
        return remote(core_out.at[slot], core_in.at[s], core_send.at[s], core_recv.at[s], (b, core))

    def pair_copies(s):
        r, c = STEPS[s]
        slot = s
        if r == 2:
            a, z = 8 + c, 12 + c
            return [
                remote(pair_out.at[slot, 0], pair_in.at[a], pair_send.at[a], pair_recv.at[a], (after, q)),
                remote(pair_out.at[slot, 1], pair_in.at[z], pair_send.at[z], pair_recv.at[z], (after, pair)),
            ]
        a = (r // 2) * 4 + c
        return [remote(pair_out.at[slot, 1], pair_in.at[a], pair_send.at[a], pair_recv.at[a], (b, pair))]

    def add_cores(s):
        r, c = STEPS[s]
        core_copy(s).wait_recv()
        mine = keep[s % 2, 0] + core_in[s, 0].astype(jnp.float32)
        theirs = keep[s % 2, 1] + core_in[s, 1].astype(jnp.float32)
        pair_out[s, 1] = theirs.astype(jnp.bfloat16)
        if r == 2:
            pair_out[s, 0] = mine.astype(jnp.bfloat16)
        else:
            total[(r // 2) * 4 + c] = mine

    def exchange(s):
        for copy in pair_copies(s):
            copy.start()

    def finish(s):
        r, c = STEPS[s]
        for copy in pair_copies(s):
            copy.wait_recv()
        if r == 2:
            lags = pair_in[8 + c].astype(jnp.float32) + pair_in[12 + c].astype(jnp.float32)
        else:
            lags = total[(r // 2) * 4 + c] + pair_in[(r // 2) * 4 + c].astype(jnp.float32)
        out[r - 1, c] = lags

    def prepare(s):
        r, c = STEPS[s]
        for p in PASS_ON.get(s, []):
            pass_on(p)
        if s == RELEASE:
            for held in range(s - 1):
                exchange(held)
        if r == 1:
            down(first, c).wait_recv()
        if r == 3:
            up(first, c).wait_recv()

    def after_cross(s, cross):
        if s >= SEND_SLOTS:
            core_copy(s - SEND_SLOTS).wait_send()
        lag_chunk(cross, table, keep.at[s % 2], core_out.at[s % SEND_SLOTS])
        core_copy(s).start()
        if s >= 1:
            add_cores(s - 1)
        if s >= RELEASE:
            exchange(s - 1)
        for done in FINISH.get(s, []):
            finish(done)

    for group in GROUPS:
        for s in group:
            prepare(s)
        owns, partners = [], []
        for s in group:
            r, c = STEPS[s]
            own = (r == 2, second if r == 2 else first)
            partner = (r == 1, c, (second if r == 1 else third).at[c])
            if own[0] not in [o[0] for o in owns]:
                owns.append(own)
            if partner[:2] not in [p[:2] for p in partners]:
                partners.append(partner)
        crosses = [cross, cross_too][:len(group)]
        cross_chunk([o[-1] for o in owns], [p[-1] for p in partners], crosses, order)
        for s, done in zip(group, crosses):
            after_cross(s, done)
    last = len(STEPS)
    add_cores(last - 1)
    exchange(last - 1)
    for s in range(max(FINISH[max(FINISH)]) + 1, last):
        finish(s)

    for c in range(CHUNKS):
        down(first, c).wait_send()
        up(first, c).wait_send()

        @pl.when(y < RING - 1)
        def _():
            far(c).wait_send()

    for s in range(last - SEND_SLOTS, last):
        core_copy(s).wait_send()
    for s in range(last):
        for copy in pair_copies(s):
            copy.wait_send()


def local(spectra, live):
    table = lag_table(lax.axis_index("frq") * BINS, BINS, F, LAGS)
    table = (table * (1.0 / math.sqrt(W))).reshape(2 * BINS, LAGS)
    block = (CHUNKS, BINS, ROWS, DEPTH)
    piece = (ROWS, ROWS, LAGS)
    half = jnp.bfloat16
    lags = pl.pallas_call(
        kernel,
        out_shape=jax.ShapeDtypeStruct((ROUNDS, CHUNKS) + piece, jnp.float32),
        in_specs=[
            pl.BlockSpec(memory_space=pltpu.VMEM),
            pl.BlockSpec(memory_space=pltpu.SMEM),
            pl.BlockSpec(memory_space=pltpu.VMEM),
        ],
        out_specs=pl.BlockSpec(memory_space=pltpu.VMEM),
        scratch_shapes=[
            pltpu.VMEM(block, half),
            pltpu.VMEM(block, half),
            pltpu.VMEM(block, half),
            pltpu.VMEM(block, half),
            pltpu.VMEM((ROWS * 2 * BINS, BLOCK), jnp.float32),
            pltpu.VMEM((ROWS * 2 * BINS, BLOCK), jnp.float32),
            pltpu.VMEM((2, 2) + piece, jnp.float32),
            pltpu.VMEM((2 * CHUNKS,) + piece, jnp.float32),
            pltpu.VMEM((SEND_SLOTS, 2) + piece, half),
            pltpu.VMEM((len(STEPS), 2) + piece, half),
            pltpu.VMEM((len(STEPS), 2) + piece, half),
            pltpu.VMEM((16,) + piece, half),
            pltpu.SemaphoreType.DMA((CHUNKS,)),
            pltpu.SemaphoreType.DMA((CHUNKS,)),
            pltpu.SemaphoreType.DMA((CHUNKS,)),
            pltpu.SemaphoreType.DMA((CHUNKS,)),
            pltpu.SemaphoreType.DMA((CHUNKS,)),
            pltpu.SemaphoreType.DMA((CHUNKS,)),
            pltpu.SemaphoreType.DMA((len(STEPS),)),
            pltpu.SemaphoreType.DMA((len(STEPS),)),
            pltpu.SemaphoreType.DMA((16,)),
            pltpu.SemaphoreType.DMA((16,)),
        ],
        compiler_params=pltpu.CompilerParams(
            collective_id=0, has_side_effects=True, vmem_limit_bytes=60 * 2**20
        ),
    )(spectra, live, table)
    return lags.reshape(ROUNDS, BLOCK, ROWS, LAGS).transpose(0, 2, 1, 3)


def solution(mesh):
    return jax.shard_map(
        local,
        mesh=mesh,
        in_specs=(P(None, "blk", None, "frq"), P("blk")),
        out_specs=P(None, ("blk", "frq"), None, None),
        check_vma=False,
    )
```
